32 devices in a mesh: shift: 4 (over y, x), sub: 8 (over z, core).
Axes of the slice: x: 2, y: 2, z: 4, core: 2. Of those that a mesh axis runs over, the one named last changes fastest.
Arguments:
- interior_rhs: bfloat16 [8, 1024, 384], P('sub'), may hold values from -6 to 6
- interface_rhs: bfloat16 [2048, 384], replicated, may hold values from -6 to 6
- interior_inverse: bfloat16 [8, 8, 1024, 1024], P('shift', 'sub'), may hold values from -0.1875 to 0.1875
- coupling: bfloat16 [8, 1024, 256], P('sub'), may hold values from -0.1875 to 0.1875
- schur_inverse: bfloat16 [8, 2048, 2048], P('shift', 'sub'), may hold values from -0.125 to 0.125
- weights: float32 [8], P('shift'), may hold values from -1 to 1
- owner_sub: int32 [8], replicated, may hold values from 0 to 7, each once
- index_blocks: int32 [8, 256], replicated, may hold values from 0 to 2047, as said below
Outputs:
- filtered: float32 [1024, 8, 384], P('shift', 'sub')
The draws below stay inside these ranges and needn't reach their ends.
Inputs may be any that keep to these rules, and one draw needn't show every extreme that they name: `index_blocks`: each row holds 256 distinct interface unknowns; of each aligned block of 2048 // 8 interface unknowns a row holds at most 64, and exactly 64 of some block. `owner_sub`: each position names a different substructure.
All inputs are finite; a program needn't handle non-finite values.
Results may differ from the reference program's by a relative error of at most 0.0053.
Values may be sent and summed in bfloat16 or wider, within the bound.
A program may use at most 64 MiB of HBM per device.

```python
import jax
import jax.numpy as jnp
from jax import lax

NI = 1024
NG = 2048
NGL = 256
COLS = 384
SHIFTS = 8
SUBS = 8
MOST = 64


def draw_index_blocks(key, part):
    block = NG // SUBS
    keys = jax.random.split(jax.random.fold_in(key, 7), SUBS)

    def one_row(single):
        first, second, third, fourth = jax.random.split(single, 4)
        full = jax.random.randint(first, (), 0, SUBS).astype(jnp.int32)
        others = jax.random.permutation(second, (SUBS - 1) * MOST)[:NGL - MOST].astype(jnp.int32)
        others = jnp.where(others >= full * MOST, others + MOST, others)
        slots = jnp.concatenate([full * MOST + jnp.arange(MOST, dtype=jnp.int32), others])
        orders = jax.vmap(lambda inner: jax.random.permutation(inner, block).astype(jnp.int32))(jax.random.split(third, SUBS))
        group = slots // MOST
        within = slots % MOST
        rows = group * block + orders[group, within]
        return rows[jax.random.permutation(fourth, NGL)]
    return jax.vmap(one_row)(keys).astype(jnp.int32)


def block_levels(own_key, extent, pieces, low, largest):
    level = 1.0
    for position, parts in pieces:
        heights = jax.random.uniform(jax.random.fold_in(jax.random.fold_in(own_key, 6), position), (parts,), jnp.float32, low / len(pieces), largest / len(pieces))
        level = level * jnp.repeat(jnp.exp(heights), extent[position] // parts).reshape((-1,) + (1,) * (len(extent) - 1 - position))
    return level


def normal_values(rng, extent, scale, reach, cuts=(), kind=jnp.bfloat16):
    array = scale * jax.random.normal(rng, extent, jnp.float32)
    if cuts:
        array = array * block_levels(rng, extent, cuts, -0.22, 0.18)
    return jnp.clip(array, -reach, reach).astype(kind)


def setup_inputs(seed: int = 0) -> dict:
    seeds = jax.random.split(jax.random.key(seed), 9)
    interior_rhs = normal_values(seeds[0], (SUBS, NI, COLS), 1.0, 6.0, ((0, 8),))
    interface_rhs = normal_values(seeds[1], (NG, COLS), 1.0, 6.0)
    interior_inverse = normal_values(seeds[2], (SHIFTS, SUBS, NI, NI), NI ** -0.5, 0.1875, ((0, 4), (1, 8)))
    coupling = normal_values(seeds[3], (SUBS, NI, NGL), NI ** -0.5, 0.1875, ((0, 8),))
    schur_inverse = normal_values(seeds[4], (SHIFTS, NG, NG), NG ** -0.5, 0.125, ((0, 4), (1, 8)))
    weights = jnp.clip(jax.random.uniform(seeds[5], (SHIFTS,), jnp.float32, -1.0, 1.0) * block_levels(seeds[5], (SHIFTS,), ((0, 4),), -0.4, 0.0), -1.0, 1.0)
    owner_sub = jax.random.permutation(seeds[6], SUBS).astype(jnp.int32)
    index_blocks = draw_index_blocks(jax.random.fold_in(seeds[8], 71), 0)
    return dict(interior_rhs=interior_rhs, interface_rhs=interface_rhs, interior_inverse=interior_inverse, coupling=coupling, schur_inverse=schur_inverse, weights=weights, owner_sub=owner_sub, index_blocks=index_blocks)


def reference(interior_rhs, interface_rhs, interior_inverse, coupling, schur_inverse, weights, owner_sub, index_blocks):
    idx = index_blocks[owner_sub]
    flat_idx = idx.reshape(-1)
    rhs_f = interior_rhs.astype(jnp.float32)
    coup_f = coupling.astype(jnp.float32)

    def one_shift(args):
        inverse, schur, weight = args
        inv_f = inverse.astype(jnp.float32)
        eliminated = jnp.einsum("sij,sjc->sic", inv_f, rhs_f).astype(jnp.bfloat16)
        coupled = jnp.einsum("sik,sic->skc", coup_f, eliminated.astype(jnp.float32)).astype(jnp.bfloat16)
        placed = jnp.zeros((NG, COLS), jnp.float32).at[flat_idx].add(coupled.reshape(-1, COLS).astype(jnp.float32))
        reduced = (interface_rhs.astype(jnp.float32) - placed).astype(jnp.bfloat16)
        interface_sol = jnp.dot(schur, reduced, preferred_element_type=jnp.float32).astype(jnp.bfloat16)
        picked = interface_sol[idx]
        correction = jnp.einsum("sik,skc->sic", coup_f, picked.astype(jnp.float32)).astype(jnp.bfloat16)
        interior_sol = eliminated.astype(jnp.float32) - jnp.einsum("sij,sjc->sic", inv_f, correction.astype(jnp.float32))
        return weight * interior_sol

    terms = lax.map(one_shift, (interior_inverse, schur_inverse, weights))
    accumulated = jnp.sum(terms, axis=0)
    return jnp.transpose(accumulated, (1, 0, 2))
```

```python
import functools

import jax
import jax.numpy as jnp
from jax import lax
from jax.experimental import pallas as pl
from jax.experimental.pallas import tpu as pltpu
from jax.sharding import PartitionSpec as P

MESH = pl.DeviceIdType.MESH
F32 = jnp.float32
BF16 = jnp.bfloat16


def dot(a, b):
    return jnp.dot(a, b, preferred_element_type=F32)


def dot_nt(a, b):
    return lax.dot_general(a, b, (((1,), (1,)), ((), ())), preferred_element_type=F32)


def ones_where(mask):
    return jnp.where(mask, 1.0, 0.0).astype(BF16)


def slot_select(index_row, start, rows, slots):
    touched = index_row.shape[1]
    hit = ones_where(lax.broadcasted_iota(jnp.int32, (rows, touched), 0) + start == index_row)
    member = dot_nt(jnp.ones((16, touched), BF16), hit)
    before = ones_where(
        lax.broadcasted_iota(jnp.int32, (rows, rows), 0)
        < lax.broadcasted_iota(jnp.int32, (rows, rows), 1)
    )
    rank = dot(member.astype(BF16), before)[0:1]
    place = jnp.where(member[0:1] > 0.5, rank, -1.0)
    chosen = ones_where(
        lax.broadcasted_iota(jnp.int32, (slots, rows), 0) == place.astype(jnp.int32)
    )
    return chosen, hit


def kernel(
    owners,
    shares,
    width,
    rhs_hbm,
    iface_hbm,
    inverse_hbm,
    couple_hbm,
    schur_hbm,
    weight_ref,
    owner_ref,
    index_ref,
    out_ref,
    rhs,
    iface,
    inverse,
    couple,
    schur,
    couple_t,
    schur_rhs,
    schur_picked,
    chosen,
    back,
    couple_slots,
    eliminated,
    gathered,
    x_send,
    x_recv,
    total,
    own_total,
    d_send,
    d_recv,
    load_sem,
    g_send,
    g_recv,
    c_send,
    c_recv,
    s_send,
    s_recv,
):
    me = lax.axis_index("sub")
    mine = lax.axis_index("shift")
    core = lax.rem(me, 2)
    sibling = me + 1 - 2 * core
    chip = me // 2
    chips = owners // 2
    shifts, rows, interface = schur.shape
    interior = rhs.shape[0]
    touched = couple.shape[1]
    slots = chosen.shape[1]
    share = interior // shares
    chunks = rhs.shape[1] // width

    loads = [
        pltpu.make_async_copy(rhs_hbm.at[0], rhs, load_sem.at[0]),
        pltpu.make_async_copy(couple_hbm.at[0], couple, load_sem.at[1]),
        pltpu.make_async_copy(schur_hbm, schur, load_sem.at[2]),
        pltpu.make_async_copy(iface_hbm, iface, load_sem.at[3]),
    ]
    inverse_loads = [
        pltpu.make_async_copy(inverse_hbm.at[j, 0], inverse.at[j], load_sem.at[4 + j])
        for j in range(shifts)
    ]
    loads[0].start()
    for load in inverse_loads:
        load.start()
    for load in loads[1:]:
        load.start()

    barrier = pltpu.get_barrier_semaphore()
    for d in range(1, owners):
        pl.semaphore_signal(
            barrier, inc=1, device_id={"sub": lax.rem(me + d, owners)}, device_id_type=MESH
        )
    for d in range(1, shares):
        pl.semaphore_signal(
            barrier, inc=1, device_id={"shift": lax.rem(mine + d, shares)}, device_id_type=MESH
        )

    def columns(c):
        return slice(c * width, (c + 1) * width)

    def block(c, source, to, way):
        return pltpu.make_async_remote_copy(
            src_ref=gathered.at[c, source],
            dst_ref=gathered.at[c, source],
            send_sem=g_send.at[c, source, way],
            recv_sem=g_recv.at[c, source],
            device_id={"sub": to},
            device_id_type=MESH,
        )

    def right(c, source):
        return block(c, source, lax.rem(me + 2, owners), 0)

    def left(c, source):
        return block(c, source, lax.rem(me + owners - 2, owners), 1)

    def across(c, source):
        return block(c, source, sibling, 2)

    def own_copies(c, act):
        @pl.when(chip < chips - 1)
        def _():
            act(right(c, me))

        @pl.when(chip > 0)
        def _():
            act(left(c, me))

        act(across(c, me))

    def hop_copies(c, hop, act, first):
        @pl.when(chip - 1 - hop >= 0)
        def _():
            source = me - 2 * (hop + 1)
            if first:
                right(c, source).wait_recv()

            @pl.when(chip < chips - 1)
            def _():
                act(right(c, source))

            act(across(c, source))

        @pl.when(chip + 1 + hop < chips)
        def _():
            source = me + 2 * (hop + 1)
            if first:
                left(c, source).wait_recv()

            @pl.when(chip > 0)
            def _():
                act(left(c, source))

            act(across(c, source))

    def start(copy):
        copy.start()

    def wait_send(copy):
        copy.wait_send()

    def send_own(c):
        own_copies(c, start)

    def hop_on(c, hop):
        if hop < chips - 1:
            hop_copies(c, hop, start, True)

    def eliminate(c):
        for j in range(shifts):
            if c == 0:
                inverse_loads[j].wait()
            solved = dot(inverse[j], rhs[:, columns(c)]).astype(BF16)
            eliminated[c, j] = solved
        if c == 0:
            loads[1].wait()
            couple_t[...] = couple[...].T
        for j in range(shifts):
            gathered[c, me, j] = dot(couple_t[...], eliminated[c, j]).astype(BF16)

    def index_row(position):
        return index_ref[pl.ds(owner_ref[position], 1), :]

    def slots_to(position, carry):
        chosen[position] = slot_select(index_row(position), me * rows, rows, slots)[0]
        return carry

    def slots_from(owner, carry):
        picks, hit = slot_select(index_row(me), owner * rows, rows, slots)
        back[owner] = dot(picks, hit).astype(BF16)
        return carry

    def pick_schur(position, carry):
        hit = ones_where(
            lax.broadcasted_iota(jnp.int32, (interface, touched), 0) == index_row(position)
        )
        flat = schur[...].reshape(shifts * rows, interface)
        schur_picked[position] = dot(flat, hit).astype(BF16)
        return carry

    def x_copy(c, to, sender):
        return pltpu.make_async_remote_copy(
            src_ref=x_send.at[c, to],
            dst_ref=x_recv.at[c, sender],
            send_sem=c_send.at[c, to],
            recv_sem=c_recv.at[c, sender],
            device_id={"sub": to},
            device_id_type=MESH,
        )

    def solve_interface(c):
        for z in range(chips):
            across(c, 2 * z + 1 - core).wait_recv()
        for j in range(shifts):
            x = schur_rhs[j, :, columns(c)]
            for p in range(owners):
                x = x - dot(schur_picked[p, j * rows : (j + 1) * rows], gathered[c, p, j])
            picked = dot(chosen[...].reshape(owners * slots, rows), x.astype(BF16))
            x_send[c, :, j] = picked.astype(BF16).reshape(owners, slots, width)

        def send(d, carry):
            to = lax.rem(me + d, owners)
            x_copy(c, to, me).start()
            return carry

        lax.fori_loop(1, owners, send, 0)
        x_recv[c, me] = x_send[c, me]

    def d_copy(c, to, sender):
        return pltpu.make_async_remote_copy(
            src_ref=d_send.at[c, to],
            dst_ref=d_recv.at[c, sender],
            send_sem=s_send.at[c, to],
            recv_sem=s_recv.at[c, sender],
            device_id={"shift": to},
            device_id_type=MESH,
        )

    def solve_interior(c):
        def receive(d, carry):
            sender = lax.rem(me + d, owners)
            x_copy(c, sender, sender).wait_recv()
            return carry

        lax.fori_loop(1, owners, receive, 0)
        acc = None
        for j in range(shifts):
            flat = x_recv[c, :, j].reshape(owners * slots, width)
            correction = dot(couple_slots[...], flat).astype(BF16)
            solved = eliminated[c, j].astype(F32) - dot(inverse[j], correction)
            term = weight_ref[j] * solved
            acc = term if acc is None else acc + term
        acc = acc.reshape(shares, share, width)
        d_send[c] = acc.astype(BF16)
        for d in range(1, shares):
            d_copy(c, lax.rem(mine + d, shares), mine).start()
        total[...] = acc
        own_total[c] = total[mine]

    def finish(c):
        acc = own_total[c]
        for d in range(1, shares):
            sender = lax.rem(mine + d, shares)
            d_copy(c, sender, sender).wait_recv()
            acc = acc + d_recv[c, sender].astype(F32)
        out_ref[:, columns(c)] = acc

    loads[0].wait()
    eliminate(0)
    pl.semaphore_wait(barrier, owners + shares - 2)
    send_own(0)

    def prepare_slots():
        lax.fori_loop(0, owners, slots_to, 0)
        lax.fori_loop(0, owners, slots_from, 0)
        couple_slots[...] = dot_nt(
            couple[...], back[...].reshape(owners * slots, touched)
        ).astype(BF16)

    def prepare_rhs():
        loads[2].wait()
        loads[3].wait()
        for j in range(shifts):
            schur_rhs[j] = dot(schur[j], iface[...])

    def prepare_schur(low, high):
        lax.fori_loop(low, high, pick_schur, 0)

    half = owners // 2
    work = [
        lambda: prepare_schur(0, half),
        lambda: prepare_schur(half, owners),
        prepare_slots,
    ]
    if chunks > 1:
        eliminate(1)
    prepare_rhs()
    steps = chunks + chips - 2
    for step in range(steps):
        for c in range(chunks):
            hop = step - c
            if 0 <= hop < chips - 1:
                hop_on(c, hop)
        complete = step - (chips - 2)
        if 0 <= complete < chunks:
            while work:
                work.pop(0)()
            solve_interface(complete)
        if step + 1 < chunks:
            send_own(step + 1)
        if step + 2 < chunks:
            eliminate(step + 2)
        if work:
            work.pop(0)()
    for c in range(chunks):
        solve_interior(c)
    for c in range(chunks):
        finish(c)

    for c in range(chunks):
        own_copies(c, wait_send)
        for hop in range(chips - 1):
            hop_copies(c, hop, wait_send, False)

        def sent(d, carry):
            to = lax.rem(me + d, owners)
            x_copy(c, to, me).wait_send()
            return carry

        lax.fori_loop(1, owners, sent, 0)
        for d in range(1, shares):
            d_copy(c, lax.rem(mine + d, shares), mine).wait_send()


def on_device(
    owners,
    shares,
    interior_rhs,
    interface_rhs,
    interior_inverse,
    coupling,
    schur_inverse,
    weights,
    owner_sub,
    index_blocks,
):
    _, interior, columns = interior_rhs.shape
    shifts, rows, interface = schur_inverse.shape
    touched = coupling.shape[2]
    slots = max(2, 2 * touched // owners)
    share = interior // shares
    width = 128
    chunks = columns // width
    whole = pl.BlockSpec(memory_space=pl.ANY)
    scalars = pl.BlockSpec(memory_space=pltpu.SMEM)
    vector = pl.BlockSpec(memory_space=pltpu.VMEM)
    result = pl.pallas_call(
        functools.partial(kernel, owners, shares, width),
        out_shape=jax.ShapeDtypeStruct((share, columns), F32),
        in_specs=[whole] * 5 + [scalars] * 2 + [vector],
        out_specs=vector,
        scratch_shapes=[
            pltpu.VMEM((interior, columns), BF16),
            pltpu.VMEM((interface, columns), BF16),
            pltpu.VMEM((shifts, interior, interior), BF16),
            pltpu.VMEM((interior, touched), BF16),
            pltpu.VMEM((shifts, rows, interface), BF16),
            pltpu.VMEM((touched, interior), BF16),
            pltpu.VMEM((shifts, rows, columns), F32),
            pltpu.VMEM((owners, shifts * rows, touched), BF16),
            pltpu.VMEM((owners, slots, rows), BF16),
            pltpu.VMEM((owners, slots, touched), BF16),
            pltpu.VMEM((interior, owners * slots), BF16),
            pltpu.VMEM((chunks, shifts, interior, width), BF16),
            pltpu.VMEM((chunks, owners, shifts, touched, width), BF16),
            pltpu.VMEM((chunks, owners, shifts, slots, width), BF16),
            pltpu.VMEM((chunks, owners, shifts, slots, width), BF16),
            pltpu.VMEM((shares, share, width), F32),
            pltpu.VMEM((chunks, share, width), F32),
            pltpu.VMEM((chunks, shares, share, width), BF16),
            pltpu.VMEM((chunks, shares, share, width), BF16),
            pltpu.SemaphoreType.DMA((4 + shifts,)),
            pltpu.SemaphoreType.DMA((chunks, owners, 3)),
            pltpu.SemaphoreType.DMA((chunks, owners)),
            pltpu.SemaphoreType.DMA((chunks, owners)),
            pltpu.SemaphoreType.DMA((chunks, owners)),
            pltpu.SemaphoreType.DMA((chunks, shares)),
            pltpu.SemaphoreType.DMA((chunks, shares)),
        ],
        compiler_params=pltpu.CompilerParams(
            collective_id=0, has_side_effects=True, vmem_limit_bytes=48 * 1024 * 1024
        ),
    )(
        interior_rhs,
        interface_rhs,
        interior_inverse,
        coupling,
        schur_inverse,
        weights,
        owner_sub,
        index_blocks,
    )
    return result[:, None, :]


def solution(mesh):
    in_specs = (
        P("sub", None, None),
        P(),
        P("shift", "sub", None, None),
        P("sub", None, None),
        P("shift", "sub", None),
        P("shift"),
        P(),
        P(),
    )
    out_specs = P("shift", "sub", None)
    body = functools.partial(on_device, mesh.shape["sub"], mesh.shape["shift"])
    return jax.shard_map(
        body, mesh=mesh, in_specs=in_specs, out_specs=out_specs, check_vma=False
    )
```

```python
import functools

import jax
import jax.numpy as jnp
from jax import lax
from jax.experimental import pallas as pl
from jax.experimental.pallas import tpu as pltpu
from jax.sharding import PartitionSpec as P

MESH = pl.DeviceIdType.MESH
F32 = jnp.float32
BF16 = jnp.bfloat16


def dot(a, b):
    return jnp.dot(a, b, preferred_element_type=F32)


def dot_nt(a, b):
    return lax.dot_general(a, b, (((1,), (1,)), ((), ())), preferred_element_type=F32)


def ones_where(mask):
    return jnp.where(mask, 1.0, 0.0).astype(BF16)


def slot_select(index_row, start, rows, slots):
    touched = index_row.shape[1]
    hit = ones_where(lax.broadcasted_iota(jnp.int32, (rows, touched), 0) + start == index_row)
    member = dot_nt(jnp.ones((16, touched), BF16), hit)
    before = ones_where(
        lax.broadcasted_iota(jnp.int32, (rows, rows), 0)
        < lax.broadcasted_iota(jnp.int32, (rows, rows), 1)
    )
    rank = dot(member.astype(BF16), before)[0:1]
    place = jnp.where(member[0:1] > 0.5, rank, -1.0)
    chosen = ones_where(
        lax.broadcasted_iota(jnp.int32, (slots, rows), 0) == place.astype(jnp.int32)
    )
    return chosen, hit


def kernel(
    owners,
    shares,
    width,
    rhs_hbm,
    iface_hbm,
    inverse_hbm,
    couple_hbm,
    schur_hbm,
    weight_ref,
    owner_ref,
    index_ref,
    out_ref,
    rhs,
    iface,
    inverse,
    couple,
    schur,
    couple_t,
    schur_rhs,
    schur_picked,
    chosen,
    back,
    couple_slots,
    eliminated,
    gathered,
    x_send,
    x_recv,
    total,
    own_total,
    d_send,
    d_recv,
    load_sem,
    g_send,
    g_recv,
    c_send,
    c_recv,
    s_send,
    s_recv,
):
    me = lax.axis_index("sub")
    mine = lax.axis_index("shift")
    core = lax.rem(me, 2)
    sibling = me + 1 - 2 * core
    chip = me // 2
    chips = owners // 2
    shifts, rows, interface = schur.shape
    interior = rhs.shape[0]
    touched = couple.shape[1]
    slots = chosen.shape[1]
    share = interior // shares
    chunks = rhs.shape[1] // width

    loads = [
        pltpu.make_async_copy(rhs_hbm.at[0], rhs, load_sem.at[0]),
        pltpu.make_async_copy(couple_hbm.at[0], couple, load_sem.at[1]),
        pltpu.make_async_copy(schur_hbm, schur, load_sem.at[2]),
        pltpu.make_async_copy(iface_hbm, iface, load_sem.at[3]),
    ]
    inverse_loads = [
        pltpu.make_async_copy(inverse_hbm.at[j, 0], inverse.at[j], load_sem.at[4 + j])
        for j in range(shifts)
    ]
    loads[0].start()
    for load in inverse_loads:
        load.start()
    for load in loads[1:]:
        load.start()

    barrier = pltpu.get_barrier_semaphore()
    for d in range(1, owners):
        pl.semaphore_signal(
            barrier, inc=1, device_id={"sub": lax.rem(me + d, owners)}, device_id_type=MESH
        )
    for d in range(1, shares):
        pl.semaphore_signal(
            barrier, inc=1, device_id={"shift": lax.rem(mine + d, shares)}, device_id_type=MESH
        )

    def columns(c):
        return slice(c * width, (c + 1) * width)

    def block(c, source, to, way):
        return pltpu.make_async_remote_copy(
            src_ref=gathered.at[c, source],
            dst_ref=gathered.at[c, source],
            send_sem=g_send.at[c, source, way],
            recv_sem=g_recv.at[c, source],
            device_id={"sub": to},
            device_id_type=MESH,
        )

    def right(c, source):
        return block(c, source, lax.rem(me + 2, owners), 0)

    def left(c, source):
        return block(c, source, lax.rem(me + owners - 2, owners), 1)

    def across(c, source):
        return block(c, source, sibling, 2)

    def own_copies(c, act):
        @pl.when(chip < chips - 1)
        def _():
            act(right(c, me))

        @pl.when(chip > 0)
        def _():
            act(left(c, me))

        act(across(c, me))

    def hop_copies(c, hop, act, first):
        @pl.when(chip - 1 - hop >= 0)
        def _():
            source = me - 2 * (hop + 1)
            if first:
                right(c, source).wait_recv()

            @pl.when(chip < chips - 1)
            def _():
                act(right(c, source))

            act(across(c, source))

        @pl.when(chip + 1 + hop < chips)
        def _():
            source = me + 2 * (hop + 1)
            if first:
                left(c, source).wait_recv()

            @pl.when(chip > 0)
            def _():
                act(left(c, source))

            act(across(c, source))

    def start(copy):
        copy.start()

    def wait_send(copy):
        copy.wait_send()

    def send_own(c):
        own_copies(c, start)

    def hop_on(c, hop):
        if hop < chips - 1:
            hop_copies(c, hop, start, True)

    def eliminate(c):
        for j in range(shifts):
            if c == 0:
                inverse_loads[j].wait()
            solved = dot(inverse[j], rhs[:, columns(c)]).astype(BF16)
            eliminated[c, j] = solved
        if c == 0:
            loads[1].wait()
            couple_t[...] = couple[...].T
        for j in range(shifts):
            gathered[c, me, j] = dot(couple_t[...], eliminated[c, j]).astype(BF16)

    def index_row(position):
        return index_ref[pl.ds(owner_ref[position], 1), :]

    def slots_to(position, carry):
        chosen[position] = slot_select(index_row(position), me * rows, rows, slots)[0]
        return carry

    def slots_from(owner, carry):
        picks, hit = slot_select(index_row(me), owner * rows, rows, slots)
        back[owner] = dot(picks, hit).astype(BF16)
        return carry

    def pick_schur(position, carry):
        hit = ones_where(
            lax.broadcasted_iota(jnp.int32, (interface, touched), 0) == index_row(position)
        )
        flat = schur[...].reshape(shifts * rows, interface)
        schur_picked[position] = dot(flat, hit).astype(BF16)
        return carry

    def x_copy(c, to, sender):
        return pltpu.make_async_remote_copy(
            src_ref=x_send.at[c, to],
            dst_ref=x_recv.at[c, sender],
            send_sem=c_send.at[c, to],
            recv_sem=c_recv.at[c, sender],
            device_id={"sub": to},
            device_id_type=MESH,
        )

    def solve_interface(c):
        for z in range(chips):
            across(c, 2 * z + 1 - core).wait_recv()
        for j in range(shifts):
            x = schur_rhs[j, :, columns(c)]
            for p in range(owners):
                x = x - dot(schur_picked[p, j * rows : (j + 1) * rows], gathered[c, p, j])
            picked = dot(chosen[...].reshape(owners * slots, rows), x.astype(BF16))
            x_send[c, :, j] = picked.astype(BF16).reshape(owners, slots, width)

        def send(d, carry):
            to = lax.rem(me + d, owners)
            x_copy(c, to, me).start()
            return carry

        lax.fori_loop(1, owners, send, 0)
        x_recv[c, me] = x_send[c, me]

    def d_copy(c, to, sender):
        return pltpu.make_async_remote_copy(
            src_ref=d_send.at[c, to],
            dst_ref=d_recv.at[c, sender],
            send_sem=s_send.at[c, to],
            recv_sem=s_recv.at[c, sender],
            device_id={"shift": to},
            device_id_type=MESH,
        )

    def solve_interior(c):
        def receive(d, carry):
            sender = lax.rem(me + d, owners)
            x_copy(c, sender, sender).wait_recv()
            return carry

        lax.fori_loop(1, owners, receive, 0)
        acc = None
        for j in range(shifts):
            flat = x_recv[c, :, j].reshape(owners * slots, width)
            correction = dot(couple_slots[...], flat).astype(BF16)
            solved = eliminated[c, j].astype(F32) - dot(inverse[j], correction)
            term = weight_ref[j] * solved
            acc = term if acc is None else acc + term
        acc = acc.reshape(shares, share, width)
        d_send[c] = acc.astype(BF16)
        for d in range(1, shares):
            d_copy(c, lax.rem(mine + d, shares), mine).start()
        total[...] = acc
        own_total[c] = total[mine]

    def finish(c):
        acc = own_total[c]
        for d in range(1, shares):
            sender = lax.rem(mine + d, shares)
            d_copy(c, sender, sender).wait_recv()
            acc = acc + d_recv[c, sender].astype(F32)
        out_ref[:, columns(c)] = acc

    loads[0].wait()
    eliminate(0)
    pl.semaphore_wait(barrier, owners + shares - 2)
    send_own(0)

    def prepare_slots():
        lax.fori_loop(0, owners, slots_to, 0, unroll=4)

    def prepare_back():
        lax.fori_loop(0, owners, slots_from, 0, unroll=4)
        couple_slots[...] = dot_nt(
            couple[...], back[...].reshape(owners * slots, touched)
        ).astype(BF16)

    def prepare_rhs():
        loads[2].wait()
        loads[3].wait()
        for j in range(shifts):
            schur_rhs[j] = dot(schur[j], iface[...])

    def prepare_schur(low, high):
        lax.fori_loop(low, high, pick_schur, 0)

    half = owners // 2
    work = [
        prepare_slots,
        lambda: prepare_schur(0, half),
        lambda: prepare_schur(half, owners),
    ]
    if chunks > 1:
        eliminate(1)
    prepare_rhs()
    steps = chunks + chips - 2
    for step in range(steps):
        for c in range(chunks):
            hop = step - c
            if 0 <= hop < chips - 1:
                hop_on(c, hop)
        complete = step - (chips - 2)
        if 0 <= complete < chunks:
            while work:
                work.pop(0)()
            solve_interface(complete)
        if step + 1 < chunks:
            send_own(step + 1)
        if step + 2 < chunks:
            eliminate(step + 2)
        if work:
            work.pop(0)()
    prepare_back()
    for c in range(chunks):
        solve_interior(c)
    for c in range(chunks):
        finish(c)

    for c in range(chunks):
        own_copies(c, wait_send)
        for hop in range(chips - 1):
            hop_copies(c, hop, wait_send, False)

        def sent(d, carry):
            to = lax.rem(me + d, owners)
            x_copy(c, to, me).wait_send()
            return carry

        lax.fori_loop(1, owners, sent, 0)
        for d in range(1, shares):
            d_copy(c, lax.rem(mine + d, shares), mine).wait_send()


def on_device(
    owners,
    shares,
    interior_rhs,
    interface_rhs,
    interior_inverse,
    coupling,
    schur_inverse,
    weights,
    owner_sub,
    index_blocks,
):
    _, interior, columns = interior_rhs.shape
    shifts, rows, interface = schur_inverse.shape
    touched = coupling.shape[2]
    slots = max(2, 2 * touched // owners)
    share = interior // shares
    width = 128
    chunks = columns // width
    whole = pl.BlockSpec(memory_space=pltpu.HBM)
    scalars = pl.BlockSpec(memory_space=pltpu.SMEM)
    vector = pl.BlockSpec(memory_space=pltpu.VMEM)
    result = pl.pallas_call(
        functools.partial(kernel, owners, shares, width),
        out_shape=jax.ShapeDtypeStruct((share, columns), F32),
        in_specs=[whole] * 5 + [scalars] * 2 + [vector],
        out_specs=vector,
        scratch_shapes=[
            pltpu.VMEM((interior, columns), BF16),
            pltpu.VMEM((interface, columns), BF16),
            pltpu.VMEM((shifts, interior, interior), BF16),
            pltpu.VMEM((interior, touched), BF16),
            pltpu.VMEM((shifts, rows, interface), BF16),
            pltpu.VMEM((touched, interior), BF16),
            pltpu.VMEM((shifts, rows, columns), F32),
            pltpu.VMEM((owners, shifts * rows, touched), BF16),
            pltpu.VMEM((owners, slots, rows), BF16),
            pltpu.VMEM((owners, slots, touched), BF16),
            pltpu.VMEM((interior, owners * slots), BF16),
            pltpu.VMEM((chunks, shifts, interior, width), BF16),
            pltpu.VMEM((chunks, owners, shifts, touched, width), BF16),
            pltpu.VMEM((chunks, owners, shifts, slots, width), BF16),
            pltpu.VMEM((chunks, owners, shifts, slots, width), BF16),
            pltpu.VMEM((shares, share, width), F32),
            pltpu.VMEM((chunks, share, width), F32),
            pltpu.VMEM((chunks, shares, share, width), BF16),
            pltpu.VMEM((chunks, shares, share, width), BF16),
            pltpu.SemaphoreType.DMA((4 + shifts,)),
            pltpu.SemaphoreType.DMA((chunks, owners, 3)),
            pltpu.SemaphoreType.DMA((chunks, owners)),
            pltpu.SemaphoreType.DMA((chunks, owners)),
            pltpu.SemaphoreType.DMA((chunks, owners)),
            pltpu.SemaphoreType.DMA((chunks, shares)),
            pltpu.SemaphoreType.DMA((chunks, shares)),
        ],
        compiler_params=pltpu.CompilerParams(
            collective_id=0, has_side_effects=True, vmem_limit_bytes=56 * 1024 * 1024
        ),
    )(
        interior_rhs,
        interface_rhs,
        interior_inverse,
        coupling,
        schur_inverse,
        weights,
        owner_sub,
        index_blocks,
    )
    return result[:, None, :]


def solution(mesh):
    in_specs = (
        P("sub", None, None),
        P(),
        P("shift", "sub", None, None),
        P("sub", None, None),
        P("shift", "sub", None),
        P("shift"),
        P(),
        P(),
    )
    out_specs = P("shift", "sub", None)
    body = functools.partial(on_device, mesh.shape["sub"], mesh.shape["shift"])
    return jax.shard_map(
        body, mesh=mesh, in_specs=in_specs, out_specs=out_specs, check_vma=False
    )
```
